1024 devices in a mesh: fsdp: 32 (over z_hi, x, core), grp: 8 (over y), rep: 4 (over z_lo).
Axes of the slice: x: 4, y: 8, z: 16 (z_hi: 4, z_lo: 4; z = z_hi * 4 + z_lo), core: 2. Of those that a mesh axis runs over, the one named last changes fastest.
Arguments:
- iterate: bfloat16 [4096, 7168], P(('fsdp', 'grp', 'rep')), may hold values from -0.040283203 to 0.040283203
Outputs:
- update: bfloat16 [4096, 7168], P('fsdp', ('grp', 'rep'))
The draws below stay inside these ranges and needn't reach their ends.
All inputs are finite; a program needn't handle non-finite values.
Results may differ from the reference program's by a relative error of at most 0.0059.
Values may be sent and summed in bfloat16 or wider, within the bound.
A program may use at most 32 MiB of HBM per device.

```python
import math
import jax
import jax.numpy as jnp
from jax import lax

COLS = 7168
ROWS = 4096


def shard_levels(own_key, extent, shards, low, high):
    factor_of = 1.0
    for axis_at, shards_of in shards:
        draws = jax.random.uniform(jax.random.fold_in(jax.random.fold_in(own_key, 6), axis_at), (shards_of,), jnp.float32, low / len(shards), high / len(shards))
        factor_of = factor_of * jnp.repeat(jnp.exp(draws), extent[axis_at] // shards_of).reshape((-1,) + (1,) * (len(extent) - 1 - axis_at))
    return factor_of


def gaussian(stream_key, extent, deviation, bound, pieces=(), kind=jnp.bfloat16):
    drawn = jax.random.normal(stream_key, extent, jnp.float32) * deviation
    if len(pieces) > 0:
        drawn = shard_levels(stream_key, extent, pieces, -0.22, 0.18) * drawn
    return jnp.clip(drawn, min=-bound, max=bound).astype(kind)


def setup_inputs(seed: int = 0) -> dict:
    key_of = jax.random.split(jax.random.key(seed), 2)
    return {
        "iterate": gaussian(key_of[0], (ROWS, COLS), (1 / (ROWS ** 0.5 + COLS ** 0.5)), 0.040283203, ((0, 1024),)),
    }


coef_linear = 3.4445
coef_cubic = -4.775
coef_quintic = 2.0315

def reference(iterate):
    gram = lax.dot_general(iterate, iterate, (((1,), (1,)), ((), ())), preferred_element_type=jnp.float32).astype(jnp.bfloat16)
    first = jnp.dot(gram, iterate, preferred_element_type=jnp.float32).astype(jnp.bfloat16)
    second = jnp.dot(gram, first, preferred_element_type=jnp.float32)
    factor = 0.2 * math.sqrt(COLS)
    combined = coef_linear * iterate.astype(jnp.float32) + coef_cubic * first.astype(jnp.float32) + coef_quintic * second
    return (factor * combined).astype(jnp.bfloat16)
```

```python
import functools
import math

import jax
import jax.numpy as jnp
from jax import lax
from jax.experimental import pallas as pl
from jax.experimental.pallas import tpu as pltpu
from jax.sharding import PartitionSpec as P

COLS = 7168

coef_linear = 3.4445
coef_cubic = -4.775
coef_quintic = 2.0315

MESH = pl.DeviceIdType.MESH
NZ, NX, NC = 4, 4, 2
NY, NL = 8, 4
OWN = 4
PIECE = NY * OWN
ROWS = NL * PIECE
WIDTH = COLS // NY
NARROW = WIDTH // NL
GROUP = NX * NC * PIECE
STRIP = ROWS // NY
Z_ORDER = (1, 3, 2)


def kernel(
    w_ref, o_ref, raw, rows32, left, panel, gram_part, gram_in, gram, first_part, first_in, first, out_part, out_in, acc,
    s_a, r_a, s_l, r_l, s_z, r_z, s_x, r_x, s_c, r_c, s_g, r_g, s_d, r_d, s_f, r_f, s_o, r_o,
):
    at = lax.axis_index("fsdp")
    y = lax.axis_index("grp")
    zl = lax.axis_index("rep")
    zh, x, c = at // (NX * NC), (at // NC) % NX, at % NC

    def far(dz=0, dx=0, dc=0, dy=0, dl=0):
        f = (((zh + dz) % NZ) * NX + (x + dx) % NX) * NC + (c + dc) % NC
        return (f, (y + dy) % NY, (zl + dl) % NL)

    partners = [far(dy=k) for k in range(1, NY)] + [far(dl=k) for k in range(1, NL)]
    partners += [far(dz=k) for k in range(1, NZ)] + [far(dx=k) for k in range(1, NX)] + [far(dc=1)]
    barrier = pltpu.get_barrier_semaphore()
    for partner in partners:
        pl.semaphore_signal(barrier, inc=1, device_id=partner, device_id_type=MESH)
    pl.semaphore_wait(barrier, len(partners))

    sent = []

    def send(src, dst, s, r, to):
        copy = pltpu.make_async_remote_copy(
            src_ref=src, dst_ref=dst, send_sem=s, recv_sem=r, device_id=to, device_id_type=MESH
        )
        copy.start()
        sent.append(copy)

    def arrived(dst, s, r):
        pltpu.make_async_remote_copy(
            src_ref=dst, dst_ref=dst, send_sem=s, recv_sem=r, device_id=far(dc=1), device_id_type=MESH
        ).wait_recv()

    for k in range(1, NY):
        to = lax.rem(y + k, NY)
        cols = pl.ds(pl.multiple_of(to * WIDTH, 128), WIDTH)
        send(w_ref.at[:, cols], raw.at[y], s_a.at[k], r_a.at[k], far(dy=k))
    raw[y] = w_ref[:, pl.ds(pl.multiple_of(y * WIDTH, 128), WIDTH)]
    for k in range(1, NY):
        arrived(raw.at[lax.rem(y + NY - k, NY)], s_a.at[k], r_a.at[k])
    for k in range(NY):
        rows32[OWN * k : OWN * (k + 1), :] = raw[k].astype(jnp.float32)
    own = rows32[...].astype(jnp.bfloat16)
    panel[0, 0, 0] = own
    left[zl] = own

    def spread_z(buf, p):
        for k in Z_ORDER:
            send(buf.at[0, 0, 0], buf.at[NZ - k, 0, 0], s_z.at[p, NZ - k], r_z.at[p, NZ - k], far(dz=k))

    def spread_x(buf, p, g):
        if g > 0:
            arrived(buf.at[g, 0, 0], s_z.at[p, g], r_z.at[p, g])
        for k in (1, 3, 2):
            send(buf.at[g, 0, 0], buf.at[g, NX - k, 0], s_x.at[p, g, NX - k], r_x.at[p, g, NX - k], far(dx=k))
        send(buf.at[g, 0, 0], buf.at[g, 0, 1], s_c.at[p, g, 0], r_c.at[p, g, 0], far(dc=1))

    def spread_c(buf, p, g):
        for k in (1, 3, 2):
            arrived(buf.at[g, k, 0], s_x.at[p, g, k], r_x.at[p, g, k])
            send(buf.at[g, k, 0], buf.at[g, k, 1], s_c.at[p, g, k], r_c.at[p, g, k], far(dc=1))

    def whole(buf, p, g):
        for k in range(NX):
            arrived(buf.at[g, k, 1], s_c.at[p, g, k], r_c.at[p, g, k])
        return buf[g].reshape(GROUP, WIDTH)

    def gram_send(g):
        part = lax.dot_general(
            left[...].reshape(ROWS, WIDTH), whole(panel, 0, g), (((1,), (1,)), ((), ())),
            preferred_element_type=jnp.float32,
        )
        gram_part[g] = part.astype(jnp.bfloat16).reshape(NY, STRIP, GROUP)
        for k in range(1, NY):
            to = lax.rem(y + k, NY)
            send(gram_part.at[g, to], gram_in.at[g, k], s_g.at[g, k], r_g.at[g, k], far(dy=k))

    def gram_sum(g):
        total = gram_part[g, y].astype(jnp.float32)
        for k in range(1, NY):
            arrived(gram_in.at[g, k], s_g.at[g, k], r_g.at[g, k])
            total = total + gram_in[g, k].astype(jnp.float32)
        gram[g, y] = total.astype(jnp.bfloat16)
        for k in range(1, NY):
            send(gram.at[g, y], gram.at[g, y], s_d.at[g, k], r_d.at[g, k], far(dy=k))

    def times(g, right, start):
        add = jnp.dot(gram[g].reshape(ROWS, GROUP), right, preferred_element_type=jnp.float32)
        if start:
            acc[...] = add
        else:
            acc[...] += add

    spread_z(panel, 0)
    for k in range(1, NL):
        send(left.at[zl], left.at[zl], s_l.at[k], r_l.at[k], far(dl=k))
    spread_x(panel, 0, 0)
    spread_x(panel, 0, 1)
    spread_x(panel, 0, 3)
    spread_c(panel, 0, 0)
    for k in range(1, NL):
        arrived(left.at[lax.rem(zl + NL - k, NL)], s_l.at[k], r_l.at[k])
    gram_send(0)
    spread_c(panel, 0, 1)
    spread_x(panel, 0, 2)
    gram_send(1)
    spread_c(panel, 0, 3)
    gram_send(3)
    gram_sum(0)
    spread_c(panel, 0, 2)
    gram_send(2)
    gram_sum(1)
    gram_sum(3)
    gram_sum(2)

    for n, g in enumerate((0, 1, 3, 2)):
        for k in range(1, NY):
            arrived(gram.at[g, lax.rem(y + NY - k, NY)], s_d.at[g, k], r_d.at[g, k])
        times(g, panel[g].reshape(GROUP, WIDTH), n == 0)
    first_part[...] = acc[...].astype(jnp.bfloat16).reshape(NL, PIECE, WIDTH)
    for k in range(1, NL):
        to = lax.rem(zl + k, NL)
        send(first_part.at[to], first_in.at[k], s_f.at[k], r_f.at[k], far(dl=k))
    total = first_part[zl].astype(jnp.float32)
    for k in range(1, NL):
        arrived(first_in.at[k], s_f.at[k], r_f.at[k])
        total = total + first_in[k].astype(jnp.float32)
    first[0, 0, 0] = total.astype(jnp.bfloat16)

    spread_z(first, 1)
    spread_x(first, 1, 0)
    spread_x(first, 1, 1)
    spread_x(first, 1, 3)
    spread_c(first, 1, 0)
    times(0, whole(first, 1, 0), True)
    spread_c(first, 1, 1)
    times(1, whole(first, 1, 1), False)
    spread_x(first, 1, 2)
    spread_c(first, 1, 3)
    times(3, whole(first, 1, 3), False)
    spread_c(first, 1, 2)
    times(2, whole(first, 1, 2), False)

    factor = 0.2 * math.sqrt(COLS)
    acc[...] = (factor * coef_quintic) * acc[...]
    mine = pl.ds(pl.multiple_of(zl * PIECE, PIECE), PIECE)
    acc[mine, :] += factor * (
        coef_linear * panel[0, 0, 0].astype(jnp.float32) + coef_cubic * first[0, 0, 0].astype(jnp.float32)
    )
    for k in range(NL):
        out_part[k] = acc[:, NARROW * k : NARROW * (k + 1)].astype(jnp.bfloat16)
    for k in range(1, NL):
        to = lax.rem(zl + k, NL)
        send(out_part.at[to], out_in.at[k], s_o.at[k], r_o.at[k], far(dl=k))
    total = out_part[zl].astype(jnp.float32)
    for k in range(1, NL):
        arrived(out_in.at[k], s_o.at[k], r_o.at[k])
        total = total + out_in[k].astype(jnp.float32)
    to_row = lax.broadcasted_iota(jnp.int32, (ROWS, ROWS), 0)
    from_row = lax.broadcasted_iota(jnp.int32, (ROWS, ROWS), 1)
    source = ((to_row // OWN) % NL) * PIECE + (to_row // (OWN * NL)) * OWN + to_row % OWN
    order = (source == from_row).astype(jnp.float32).astype(jnp.bfloat16)
    o_ref[...] = jnp.dot(order, total.astype(jnp.bfloat16), preferred_element_type=jnp.float32).astype(jnp.bfloat16)

    for copy in sent:
        copy.wait_send()


def body(iterate):
    bf, f32, dma = jnp.bfloat16, jnp.float32, pltpu.SemaphoreType.DMA
    vm = pltpu.VMEM
    counts = [(NY,), (NL,), (2, NZ), (2, NZ, NX), (2, NZ, NX), (NZ, NY), (NZ, NY), (NL,), (NL,)]
    sems = [dma(n) for n in counts for _ in range(2)]
    return pl.pallas_call(
        kernel,
        out_shape=jax.ShapeDtypeStruct((ROWS, NARROW), bf),
        in_specs=[pl.BlockSpec(memory_space=pltpu.VMEM)],
        out_specs=pl.BlockSpec(memory_space=pltpu.VMEM),
        scratch_shapes=[
            vm((NY, OWN, WIDTH), bf),
            vm((PIECE, WIDTH), f32),
            vm((NL, PIECE, WIDTH), bf),
            vm((NZ, NX, NC, PIECE, WIDTH), bf),
            vm((NZ, NY, STRIP, GROUP), bf),
            vm((NZ, NY, STRIP, GROUP), bf),
            vm((NZ, NY, STRIP, GROUP), bf),
            vm((NL, PIECE, WIDTH), bf),
            vm((NL, PIECE, WIDTH), bf),
            vm((NZ, NX, NC, PIECE, WIDTH), bf),
            vm((NL, ROWS, NARROW), bf),
            vm((NL, ROWS, NARROW), bf),
            vm((ROWS, WIDTH), f32),
        ] + sems,
        compiler_params=pltpu.CompilerParams(collective_id=0, has_side_effects=True, vmem_limit_bytes=32 << 20),
        cost_estimate=pl.CostEstimate(flops=6 * ROWS * GROUP * NZ * WIDTH, bytes_accessed=4 * ROWS * NARROW, transcendentals=0),
    )(iterate)


def solution(mesh):
    in_specs = (P(("fsdp", "grp", "rep"), None),)
    out_specs = P("fsdp", ("grp", "rep"))
    return jax.shard_map(body, mesh=mesh, in_specs=in_specs, out_specs=out_specs, check_vma=False)
```

```python
import math

import jax
import jax.numpy as jnp
from jax import lax
from jax.experimental import pallas as pl
from jax.experimental.pallas import tpu as pltpu
from jax.sharding import PartitionSpec as P

COLS = 7168

coef_linear = 3.4445
coef_cubic = -4.775
coef_quintic = 2.0315

MESH = pl.DeviceIdType.MESH
NZ, NX, NC = 4, 4, 2
NY, NL = 8, 4
OWN = 4
PIECE = NY * OWN
HALF = NL * PIECE
ROWS = NC * HALF
WIDTH = COLS // NY
NARROW = WIDTH // NL
GROUP = NX * PIECE
STRIP = ROWS // NY
AROUND = (1, 3, 2)
CHUNKS = ((0, 512), (512, 384))
LAST = len(CHUNKS) - 1
FIRST_PLAN = (
    ("x", 0, 0), ("x", 1, 0), ("x", 0, 3), ("x", 1, 1), ("x", 0, 1), ("x", 1, 3), ("u", 0, 0),
    ("u", 1, 0), ("x", 0, 2), ("x", 1, 2), ("u", 0, 1), ("u", 1, 1), ("u", 0, 3), ("u", 1, 3),
    ("s", 0, 0), ("s", 0, 1), ("u", 0, 2), ("u", 1, 2), ("s", 0, 3), ("s", 0, 2),
)
SECOND_PLAN = (
    ("x", 0, 0), ("x", 1, 0), ("x", 0, 3), ("x", 0, 1), ("u", 0, 0), ("x", 1, 1), ("x", 1, 3),
    ("u", 0, 1), ("u", 0, 3), ("x", 0, 2), ("u", 1, 0), ("x", 1, 2), ("u", 1, 1), ("u", 1, 3),
    ("u", 0, 2), ("o", 0, 0), ("u", 1, 2), ("o", 1, 0),
)
ORDER = (0, 1, 3, 2)
RELAY = ((0, 3), (1, 1))


def kernel(
    w_ref, o_ref, raw, rows32, left, panel, gram32, gram_part, gram_in, gram, pair_out, pair_in, first_part, first_in,
    first, out_all, out_part, out_in, acc, gram_acc,
    s_a, r_a, s_l, r_l, s_m, r_m, s_z, r_z, s_x, r_x, s_g, r_g, s_d, r_d, s_p, r_p, s_f, r_f, s_o, r_o,
):
    at = lax.axis_index("fsdp")
    y = lax.axis_index("grp")
    zl = lax.axis_index("rep")
    zh, x, c = lax.div(at, NX * NC), lax.rem(lax.div(at, NC), NX), lax.rem(at, NC)

    def step(start, by, size):
        return lax.rem(start + by, size)

    line_y = [(at, step(y, k, NY), zl) for k in range(NY)]
    line_l = [(at, y, step(zl, k, NL)) for k in range(NL)]
    line_x = [(zh * (NX * NC) + step(x, k, NX) * NC + c, y, zl) for k in range(NX)]
    line_z = [(step(zh, k, NZ) * (NX * NC) + x * NC + c, y, zl) for k in range(NZ)]
    other = (zh * (NX * NC) + x * NC + (1 - c), y, zl)

    partners = line_y[1:] + line_l[1:] + line_x[1:] + [line_z[1], line_z[3], other]
    barrier = pltpu.get_barrier_semaphore()
    for partner in partners:
        pl.semaphore_signal(barrier, inc=1, device_id=partner, device_id_type=MESH)
    pl.semaphore_wait(barrier, len(partners))

    sent = []

    def send(src, dst, s, r, to):
        copy = pltpu.make_async_remote_copy(
            src_ref=src, dst_ref=dst, send_sem=s, recv_sem=r, device_id=to, device_id_type=MESH
        )
        copy.start()
        sent.append(copy)

    def arrived(dst, s, r):
        pltpu.make_async_remote_copy(
            src_ref=dst, dst_ref=dst, send_sem=s, recv_sem=r, device_id=other, device_id_type=MESH
        ).wait_recv()

    def to_line(to):
        return w_ref.at[:, pl.ds(pl.multiple_of(to * WIDTH, 128), WIDTH)]

    for k in range(1, NY):
        send(to_line(step(y, k, NY)), raw.at[y], s_a.at[k], r_a.at[k], line_y[k])
    keep = pltpu.make_async_copy(to_line(y), raw.at[y], s_a.at[0])
    keep.start()
    keep.wait()
    for k in range(1, NY):
        arrived(raw.at[step(y, NY - k, NY)], s_a.at[k], r_a.at[k])
    for k in range(NY):
        rows32[OWN * k : OWN * (k + 1), :] = raw[k].astype(jnp.float32)
    own = rows32[...].astype(jnp.bfloat16)
    panel[0, 0] = own
    left[c, zl] = own

    def part(buf, g, k, n):
        return buf.at[g, k, :, pl.ds(CHUNKS[n][0], CHUNKS[n][1])]

    def z_out(buf, p, n):
        for k in (1, 3):
            send(part(buf, 0, 0, n), part(buf, NZ - k, 0, n), s_z.at[p, n, NZ - k], r_z.at[p, n, NZ - k], line_z[k])

    def spread(buf, p, plan, use, rest):
        for what, n, g in plan:
            if what == "x":
                if g > 0:
                    arrived(part(buf, g, 0, n), s_z.at[p, n, g], r_z.at[p, n, g])
                if (n, g) in RELAY:
                    send(part(buf, g, 0, n), part(buf, 2, 0, n), s_z.at[p, n, 2], r_z.at[p, n, 2], line_z[NZ - g])
                for k in AROUND:
                    to = NX - k
                    send(part(buf, g, 0, n), part(buf, g, to, n), s_x.at[p, n, g, to], r_x.at[p, n, g, to], line_x[k])
            elif what == "u":
                for k in AROUND:
                    arrived(part(buf, g, k, n), s_x.at[p, n, g, k], r_x.at[p, n, g, k])
                use(n, g)
            else:
                rest(n, g)

    def columns(buf, g, n):
        return buf[g, :, :, CHUNKS[n][0] : CHUNKS[n][0] + CHUNKS[n][1]].reshape(GROUP, CHUNKS[n][1])

    def gram_step(n, g):
        if (n, g) == (0, 0):
            for k in range(1, NL):
                who = step(zl, NL - k, NL)
                arrived(left.at[c, who], s_l.at[k], r_l.at[k])
                send(left.at[c, who], left.at[c, who], s_m.at[k], r_m.at[k], other)
            for k in range(NL):
                arrived(left.at[1 - c, step(zl, NL - k, NL)], s_m.at[k], r_m.at[k])
        lo, size = CHUNKS[n]
        add = lax.dot_general(
            left[:, :, :, lo : lo + size].reshape(ROWS, size), columns(panel, g, n), (((1,), (1,)), ((), ())),
            preferred_element_type=jnp.float32,
        )
        if n < LAST:
            gram_acc[...] = add if n == 0 else gram_acc[...] + add
            return
        total = (gram_acc[...] + add).reshape(NY, STRIP, GROUP)
        gram32[g] = total
        gram_part[g] = total.astype(jnp.bfloat16)
        for k in range(1, NY):
            send(gram_part.at[g, step(y, k, NY)], gram_in.at[g, k], s_g.at[g, k], r_g.at[g, k], line_y[k])

    def gram_sum(n, g):
        total = gram32[g, y]
        for k in range(1, NY):
            arrived(gram_in.at[g, k], s_g.at[g, k], r_g.at[g, k])
            total = total + gram_in[g, k].astype(jnp.float32)
        gram[g, y] = total.astype(jnp.bfloat16)
        for k in range(1, NY):
            send(gram.at[g, y], gram.at[g, y], s_d.at[g, k], r_d.at[g, k], line_y[k])

    def times(buf, n, g):
        add = jnp.dot(gram[g].reshape(ROWS, GROUP), columns(buf, g, n), preferred_element_type=jnp.float32)
        lo, size = CHUNKS[n]
        if g == ORDER[0]:
            acc[:, lo : lo + size] = add
        else:
            acc[:, lo : lo + size] += add

    half = pl.ds(pl.multiple_of(c * HALF, HALF), HALF)
    other_half = pl.ds(pl.multiple_of((1 - c) * HALF, HALF), HALF)
    mine = pl.ds(pl.multiple_of(c * HALF + zl * PIECE, PIECE), PIECE)

    def pair_send(p, n):
        lo, size = CHUNKS[n]
        cut = pl.ds(lo, size)
        pair_out[p, :, lo : lo + size] = acc[other_half, lo : lo + size].astype(jnp.bfloat16)
        send(pair_out.at[p, :, cut], pair_in.at[p, :, cut], s_p.at[p, n], r_p.at[p, n], other)

    def pair_add(p, n):
        lo, size = CHUNKS[n]
        arrived(pair_in.at[p, :, pl.ds(lo, size)], s_p.at[p, n], r_p.at[p, n])
        acc[half, lo : lo + size] += pair_in[p, :, lo : lo + size].astype(jnp.float32)

    for n in range(len(CHUNKS)):
        z_out(panel, 0, n)
    send(left.at[c, zl], left.at[c, zl], s_m.at[0], r_m.at[0], other)
    for k in range(1, NL):
        send(left.at[c, zl], left.at[c, zl], s_l.at[k], r_l.at[k], line_l[k])
    spread(panel, 0, FIRST_PLAN, gram_step, gram_sum)

    for g in ORDER:
        for k in range(1, NY):
            arrived(gram.at[g, step(y, NY - k, NY)], s_d.at[g, k], r_d.at[g, k])
        for n in range(len(CHUNKS)):
            times(panel, n, g)
            if g == ORDER[-1]:
                pair_send(0, n)
    for n, (lo, size) in enumerate(CHUNKS):
        pair_add(0, n)
        cut = pl.ds(lo, size)
        first_part[:, :, lo : lo + size] = acc[half, lo : lo + size].astype(jnp.bfloat16).reshape(NL, PIECE, size)
        for k in range(1, NL):
            to = first_part.at[step(zl, k, NL), :, cut]
            send(to, first_in.at[k, :, cut], s_f.at[n, k], r_f.at[n, k], line_l[k])
    for n, (lo, size) in enumerate(CHUNKS):
        total = acc[mine, lo : lo + size]
        for k in range(1, NL):
            arrived(first_in.at[k, :, pl.ds(lo, size)], s_f.at[n, k], r_f.at[n, k])
            total = total + first_in[k, :, lo : lo + size].astype(jnp.float32)
        first[0, 0, :, lo : lo + size] = total.astype(jnp.bfloat16)
        z_out(first, 1, n)

    factor = 0.2 * math.sqrt(COLS)

    def second_step(n, g):
        times(first, n, g)
        if g == ORDER[-1]:
            pair_send(1, n)

    def out_step(n, g):
        pair_add(1, n)
        lo, size = CHUNKS[n]
        acc[mine, lo : lo + size] += (coef_linear / coef_quintic) * panel[0, 0, :, lo : lo + size].astype(jnp.float32) + (
            coef_cubic / coef_quintic
        ) * first[0, 0, :, lo : lo + size].astype(jnp.float32)
        out_all[:, lo : lo + size] = ((factor * coef_quintic) * acc[half, lo : lo + size]).astype(jnp.bfloat16)
        for q in range(NL):
            if lo < NARROW * (q + 1) <= lo + size:
                out_part[q] = out_all[:, NARROW * q : NARROW * (q + 1)]

                @pl.when(zl != q)
                def _():
                    pltpu.make_async_remote_copy(
                        src_ref=out_part.at[q], dst_ref=out_in.at[zl], send_sem=s_o.at[q], recv_sem=r_o.at[zl],
                        device_id=(at, y, q), device_id_type=MESH,
                    ).start()

    spread(first, 1, SECOND_PLAN, second_step, out_step)
    total = out_part[zl].astype(jnp.float32)
    for k in range(1, NL):
        who = step(zl, NL - k, NL)
        arrived(out_in.at[who], s_o.at[who], r_o.at[who])
        total = total + out_in[who].astype(jnp.float32)
    to_row = lax.broadcasted_iota(jnp.int32, (HALF, HALF), 0)
    from_row = lax.broadcasted_iota(jnp.int32, (HALF, HALF), 1)
    source = ((to_row // OWN) % NL) * PIECE + (to_row // (OWN * NL)) * OWN + to_row % OWN
    order = (source == from_row).astype(jnp.float32).astype(jnp.bfloat16)
    o_ref[...] = jnp.dot(order, total.astype(jnp.bfloat16), preferred_element_type=jnp.float32).astype(jnp.bfloat16)

    for k in range(1, NL):
        who = step(zl, k, NL)
        pltpu.make_async_remote_copy(
            src_ref=out_part.at[who], dst_ref=out_in.at[zl], send_sem=s_o.at[who], recv_sem=r_o.at[zl],
            device_id=(at, y, who), device_id_type=MESH,
        ).wait_send()
    for copy in sent:
        copy.wait_send()


def body(iterate):
    bf, f32, dma = jnp.bfloat16, jnp.float32, pltpu.SemaphoreType.DMA
    vm = pltpu.VMEM
    n = len(CHUNKS)
    counts = [(NY,), (NL,), (NL,), (2, n, NZ), (2, n, NZ, NX), (NZ, NY), (NZ, NY), (2, n), (n, NL), (NL,)]
    sems = [dma(count) for count in counts for _ in range(2)]
    return pl.pallas_call(
        kernel,
        out_shape=jax.ShapeDtypeStruct((HALF, NARROW), bf),
        in_specs=[pl.BlockSpec(memory_space=pl.ANY)],
        out_specs=pl.BlockSpec(memory_space=pltpu.VMEM),
        scratch_shapes=[
            vm((NY, OWN, WIDTH), bf),
            vm((PIECE, WIDTH), f32),
            vm((NC, NL, PIECE, WIDTH), bf),
            vm((NZ, NX, PIECE, WIDTH), bf),
            vm((NZ, NY, STRIP, GROUP), f32),
            vm((NZ, NY, STRIP, GROUP), bf),
            vm((NZ, NY, STRIP, GROUP), bf),
            vm((NZ, NY, STRIP, GROUP), bf),
            vm((2, HALF, WIDTH), bf),
            vm((2, HALF, WIDTH), bf),
            vm((NL, PIECE, WIDTH), bf),
            vm((NL, PIECE, WIDTH), bf),
            vm((NZ, NX, PIECE, WIDTH), bf),
            vm((HALF, WIDTH), bf),
            vm((NL, HALF, NARROW), bf),
            vm((NL, HALF, NARROW), bf),
            vm((ROWS, WIDTH), f32),
            vm((ROWS, GROUP), f32),
        ] + sems,
        compiler_params=pltpu.CompilerParams(collective_id=0, has_side_effects=True, vmem_limit_bytes=32 << 20),
        cost_estimate=pl.CostEstimate(flops=6 * ROWS * GROUP * NZ * WIDTH, bytes_accessed=4 * HALF * NARROW, transcendentals=0),
    )(iterate)


def solution(mesh):
    in_specs = (P(("fsdp", "grp", "rep"), None),)
    out_specs = P("fsdp", ("grp", "rep"))
    return jax.shard_map(body, mesh=mesh, in_specs=in_specs, out_specs=out_specs, check_vma=False)
```

```python
import math

import jax
import jax.numpy as jnp
from jax import lax
from jax.experimental import pallas as pl
from jax.experimental.pallas import tpu as pltpu
from jax.sharding import PartitionSpec as P

COLS = 7168

coef_linear = 3.4445
coef_cubic = -4.775
coef_quintic = 2.0315

MESH = pl.DeviceIdType.MESH
NZ, NX, NC = 4, 4, 2
NY, NL = 8, 4
OWN = 4
PIECE = NY * OWN
HALF = NL * PIECE
ROWS = NC * HALF
WIDTH = COLS // NY
NARROW = WIDTH // NL
GROUP = NX * PIECE
STRIP = ROWS // NY
AROUND = (2, 1, 3)
CHUNKS = ((0, 512), (512, 384))
LAST = len(CHUNKS) - 1
FIRST_PLAN = (
    ("x", 0, 0), ("x", 1, 0), ("x", 0, 3), ("x", 1, 1), ("x", 0, 1), ("x", 1, 3), ("u", 0, 0),
    ("u", 1, 0), ("x", 0, 2), ("x", 1, 2), ("u", 0, 1), ("u", 1, 1), ("u", 0, 3), ("u", 1, 3),
    ("s", 0, 0), ("s", 0, 1), ("u", 0, 2), ("u", 1, 2), ("s", 0, 3), ("s", 0, 2),
)
SECOND_PLAN = (
    ("x", 0, 0), ("x", 1, 0), ("x", 0, 3), ("x", 0, 1), ("u", 0, 0), ("x", 1, 1), ("x", 1, 3),
    ("u", 0, 1), ("u", 0, 3), ("x", 0, 2), ("u", 1, 0), ("x", 1, 2), ("u", 1, 1), ("u", 1, 3),
    ("u", 0, 2), ("o", 0, 0), ("u", 1, 2), ("o", 1, 0),
)
ORDER = (0, 1, 3, 2)
RELAY = ((0, 3), (1, 1))


def kernel(
    w_ref, o_ref, raw, rows32, left, panel, gram32, gram_part, gram_in, gram, pair_out, pair_in, first_part, first_in,
    first, out_all, out_part, out_in, acc, gram_acc,
    s_a, r_a, s_l, r_l, s_m, r_m, s_z, r_z, s_x, r_x, s_g, r_g, s_d, r_d, s_p, r_p, s_f, r_f, s_o, r_o,
):
    at = lax.axis_index("fsdp")
    y = lax.axis_index("grp")
    zl = lax.axis_index("rep")
    zh, x, c = lax.div(at, NX * NC), lax.rem(lax.div(at, NC), NX), lax.rem(at, NC)

    def step(start, by, size):
        return lax.rem(start + by, size)

    line_y = [(at, step(y, k, NY), zl) for k in range(NY)]
    line_l = [(at, y, step(zl, k, NL)) for k in range(NL)]
    line_x = [(zh * (NX * NC) + step(x, k, NX) * NC + c, y, zl) for k in range(NX)]
    line_z = [(step(zh, k, NZ) * (NX * NC) + x * NC + c, y, zl) for k in range(NZ)]
    other = (zh * (NX * NC) + x * NC + (1 - c), y, zl)

    partners = line_y[1:] + line_l[1:] + line_x[1:] + [line_z[1], line_z[3], other]
    barrier = pltpu.get_barrier_semaphore()
    for partner in partners:
        pl.semaphore_signal(barrier, inc=1, device_id=partner, device_id_type=MESH)
    pl.semaphore_wait(barrier, len(partners))

    sent = []

    def send(src, dst, s, r, to):
        copy = pltpu.make_async_remote_copy(
            src_ref=src, dst_ref=dst, send_sem=s, recv_sem=r, device_id=to, device_id_type=MESH
        )
        copy.start()
        sent.append(copy)

    def arrived(dst, s, r):
        pltpu.make_async_remote_copy(
            src_ref=dst, dst_ref=dst, send_sem=s, recv_sem=r, device_id=other, device_id_type=MESH
        ).wait_recv()

    def to_line(to):
        return w_ref.at[:, pl.ds(pl.multiple_of(to * WIDTH, 128), WIDTH)]

    for k in (4, 3, 5, 2, 6, 1, 7):
        send(to_line(step(y, k, NY)), raw.at[y], s_a.at[k], r_a.at[k], line_y[k])
    keep = pltpu.make_async_copy(to_line(y), raw.at[y], s_a.at[0])
    keep.start()
    keep.wait()
    for k in range(1, NY):
        arrived(raw.at[step(y, NY - k, NY)], s_a.at[k], r_a.at[k])
    for k in range(NY):
        rows32[OWN * k : OWN * (k + 1), :] = raw[k].astype(jnp.float32)
    own = rows32[...].astype(jnp.bfloat16)
    panel[0, 0] = own
    left[c, zl] = own

    def part(buf, g, k, n):
        return buf.at[g, k, :, pl.ds(CHUNKS[n][0], CHUNKS[n][1])]

    def z_out(buf, p, n):
        for k in ((1, 3), (3, 1))[n]:
            send(part(buf, 0, 0, n), part(buf, NZ - k, 0, n), s_z.at[p, n, NZ - k], r_z.at[p, n, NZ - k], line_z[k])

    def spread(buf, p, plan, use, rest):
        for what, n, g in plan:
            if what == "x":
                if g > 0:
                    arrived(part(buf, g, 0, n), s_z.at[p, n, g], r_z.at[p, n, g])
                if (n, g) in RELAY:
                    send(part(buf, g, 0, n), part(buf, 2, 0, n), s_z.at[p, n, 2], r_z.at[p, n, 2], line_z[NZ - g])
                for k in AROUND:
                    to = NX - k
                    send(part(buf, g, 0, n), part(buf, g, to, n), s_x.at[p, n, g, to], r_x.at[p, n, g, to], line_x[k])
            elif what == "u":
                for k in AROUND:
                    arrived(part(buf, g, k, n), s_x.at[p, n, g, k], r_x.at[p, n, g, k])
                use(n, g)
            else:
                rest(n, g)

    def columns(buf, g, n):
        return buf[g, :, :, CHUNKS[n][0] : CHUNKS[n][0] + CHUNKS[n][1]].reshape(GROUP, CHUNKS[n][1])

    def gram_step(n, g):
        if (n, g) == (0, 0):
            for k in range(1, NL):
                who = step(zl, NL - k, NL)
                arrived(left.at[c, who], s_l.at[k], r_l.at[k])
                send(left.at[c, who], left.at[c, who], s_m.at[k], r_m.at[k], other)
            for k in range(NL):
                arrived(left.at[1 - c, step(zl, NL - k, NL)], s_m.at[k], r_m.at[k])
        lo, size = CHUNKS[n]
        add = lax.dot_general(
            left[:, :, :, lo : lo + size].reshape(ROWS, size), columns(panel, g, n), (((1,), (1,)), ((), ())),
            preferred_element_type=jnp.float32,
        )
        if n < LAST:
            gram_acc[...] = add if n == 0 else gram_acc[...] + add
            return
        total = (gram_acc[...] + add).reshape(NY, STRIP, GROUP)
        gram32[g] = total
        gram_part[g] = total.astype(jnp.bfloat16)
        for k in (4, 3, 5, 2, 6, 1, 7):
            send(gram_part.at[g, step(y, k, NY)], gram_in.at[g, k], s_g.at[g, k], r_g.at[g, k], line_y[k])

    def gram_sum(n, g):
        total = gram32[g, y]
        for k in range(1, NY):
            arrived(gram_in.at[g, k], s_g.at[g, k], r_g.at[g, k])
            total = total + gram_in[g, k].astype(jnp.float32)
        gram[g, y] = total.astype(jnp.bfloat16)
        for k in (4, 3, 5, 2, 6, 1, 7):
            send(gram.at[g, y], gram.at[g, y], s_d.at[g, k], r_d.at[g, k], line_y[k])

    def times(buf, n, g):
        add = jnp.dot(gram[g].reshape(ROWS, GROUP), columns(buf, g, n), preferred_element_type=jnp.float32)
        lo, size = CHUNKS[n]
        if g == ORDER[0]:
            acc[:, lo : lo + size] = add
        else:
            acc[:, lo : lo + size] += add

    half = pl.ds(pl.multiple_of(c * HALF, HALF), HALF)
    other_half = pl.ds(pl.multiple_of((1 - c) * HALF, HALF), HALF)
    mine = pl.ds(pl.multiple_of(c * HALF + zl * PIECE, PIECE), PIECE)

    def pair_send(p, n):
        lo, size = CHUNKS[n]
        cut = pl.ds(lo, size)
        pair_out[p, :, lo : lo + size] = acc[other_half, lo : lo + size].astype(jnp.bfloat16)
        send(pair_out.at[p, :, cut], pair_in.at[p, :, cut], s_p.at[p, n], r_p.at[p, n], other)

    def pair_add(p, n):
        lo, size = CHUNKS[n]
        arrived(pair_in.at[p, :, pl.ds(lo, size)], s_p.at[p, n], r_p.at[p, n])
        acc[half, lo : lo + size] += pair_in[p, :, lo : lo + size].astype(jnp.float32)

    for n in range(len(CHUNKS)):
        z_out(panel, 0, n)
    send(left.at[c, zl], left.at[c, zl], s_m.at[0], r_m.at[0], other)
    for k in range(1, NL):
        send(left.at[c, zl], left.at[c, zl], s_l.at[k], r_l.at[k], line_l[k])
    spread(panel, 0, FIRST_PLAN, gram_step, gram_sum)

    for g in ORDER:
        for k in range(1, NY):
            arrived(gram.at[g, step(y, NY - k, NY)], s_d.at[g, k], r_d.at[g, k])
        for n in range(len(CHUNKS)):
            times(panel, n, g)
            if g == ORDER[-1]:
                pair_send(0, n)
    for n, (lo, size) in enumerate(CHUNKS):
        pair_add(0, n)
        cut = pl.ds(lo, size)
        first_part[:, :, lo : lo + size] = acc[half, lo : lo + size].astype(jnp.bfloat16).reshape(NL, PIECE, size)
        for k in range(1, NL):
            to = first_part.at[step(zl, k, NL), :, cut]
            send(to, first_in.at[k, :, cut], s_f.at[n, k], r_f.at[n, k], line_l[k])
    for n, (lo, size) in enumerate(CHUNKS):
        total = acc[mine, lo : lo + size]
        for k in range(1, NL):
            arrived(first_in.at[k, :, pl.ds(lo, size)], s_f.at[n, k], r_f.at[n, k])
            total = total + first_in[k, :, lo : lo + size].astype(jnp.float32)
        first[0, 0, :, lo : lo + size] = total.astype(jnp.bfloat16)
        z_out(first, 1, n)

    factor = 0.2 * math.sqrt(COLS)

    def second_step(n, g):
        times(first, n, g)
        if g == ORDER[-1]:
            pair_send(1, n)

    def out_step(n, g):
        pair_add(1, n)
        lo, size = CHUNKS[n]
        acc[mine, lo : lo + size] += (coef_linear / coef_quintic) * panel[0, 0, :, lo : lo + size].astype(jnp.float32) + (
            coef_cubic / coef_quintic
        ) * first[0, 0, :, lo : lo + size].astype(jnp.float32)
        out_all[:, lo : lo + size] = ((factor * coef_quintic) * acc[half, lo : lo + size]).astype(jnp.bfloat16)
        for q in range(NL):
            if lo < NARROW * (q + 1) <= lo + size:
                out_part[q] = out_all[:, NARROW * q : NARROW * (q + 1)]

                @pl.when(zl != q)
                def _():
                    pltpu.make_async_remote_copy(
                        src_ref=out_part.at[q], dst_ref=out_in.at[zl], send_sem=s_o.at[q], recv_sem=r_o.at[zl],
                        device_id=(at, y, q), device_id_type=MESH,
                    ).start()

    spread(first, 1, SECOND_PLAN, second_step, out_step)
    total = out_part[zl].astype(jnp.float32)
    for k in range(1, NL):
        who = step(zl, NL - k, NL)
        arrived(out_in.at[who], s_o.at[who], r_o.at[who])
        total = total + out_in[who].astype(jnp.float32)
    to_row = lax.broadcasted_iota(jnp.int32, (HALF, HALF), 0)
    from_row = lax.broadcasted_iota(jnp.int32, (HALF, HALF), 1)
    source = ((to_row // OWN) % NL) * PIECE + (to_row // (OWN * NL)) * OWN + to_row % OWN
    order = (source == from_row).astype(jnp.float32).astype(jnp.bfloat16)
    o_ref[...] = jnp.dot(order, total.astype(jnp.bfloat16), preferred_element_type=jnp.float32).astype(jnp.bfloat16)

    for k in range(1, NL):
        who = step(zl, k, NL)
        pltpu.make_async_remote_copy(
            src_ref=out_part.at[who], dst_ref=out_in.at[zl], send_sem=s_o.at[who], recv_sem=r_o.at[zl],
            device_id=(at, y, who), device_id_type=MESH,
        ).wait_send()
    for copy in sent:
        copy.wait_send()


def body(iterate):
    bf, f32, dma = jnp.bfloat16, jnp.float32, pltpu.SemaphoreType.DMA
    vm = pltpu.VMEM
    n = len(CHUNKS)
    counts = [(NY,), (NL,), (NL,), (2, n, NZ), (2, n, NZ, NX), (NZ, NY), (NZ, NY), (2, n), (n, NL), (NL,)]
    sems = [dma(count) for count in counts for _ in range(2)]
    return pl.pallas_call(
        kernel,
        out_shape=jax.ShapeDtypeStruct((HALF, NARROW), bf),
        in_specs=[pl.BlockSpec(memory_space=pl.ANY)],
        out_specs=pl.BlockSpec(memory_space=pltpu.VMEM),
        scratch_shapes=[
            vm((NY, OWN, WIDTH), bf),
            vm((PIECE, WIDTH), f32),
            vm((NC, NL, PIECE, WIDTH), bf),
            vm((NZ, NX, PIECE, WIDTH), bf),
            vm((NZ, NY, STRIP, GROUP), f32),
            vm((NZ, NY, STRIP, GROUP), bf),
            vm((NZ, NY, STRIP, GROUP), bf),
            vm((NZ, NY, STRIP, GROUP), bf),
            vm((2, HALF, WIDTH), bf),
            vm((2, HALF, WIDTH), bf),
            vm((NL, PIECE, WIDTH), bf),
            vm((NL, PIECE, WIDTH), bf),
            vm((NZ, NX, PIECE, WIDTH), bf),
            vm((HALF, WIDTH), bf),
            vm((NL, HALF, NARROW), bf),
            vm((NL, HALF, NARROW), bf),
            vm((ROWS, WIDTH), f32),
            vm((ROWS, GROUP), f32),
        ] + sems,
        compiler_params=pltpu.CompilerParams(collective_id=0, has_side_effects=True, vmem_limit_bytes=32 << 20),
        cost_estimate=pl.CostEstimate(flops=6 * ROWS * GROUP * NZ * WIDTH, bytes_accessed=4 * HALF * NARROW, transcendentals=0),
    )(iterate)


def solution(mesh):
    in_specs = (P(("fsdp", "grp", "rep"), None),)
    out_specs = P("fsdp", ("grp", "rep"))
    return jax.shard_map(body, mesh=mesh, in_specs=in_specs, out_specs=out_specs, check_vma=False)
```
